256 devices in a mesh: grp: 8 (over x, z_lo), freq: 32 (over y, z_hi, core).
Axes of the slice: x: 4, y: 4, z: 8 (z_hi: 4, z_lo: 2; z = z_hi * 2 + z_lo), core: 2. Of those that a mesh axis runs over, the one named last changes fastest.
Arguments:
- samples: int32 [1024, 268288], P(('grp', 'freq')), may hold values from -128 to 127
- window: float32 [4, 2048], replicated, may hold values from 0.2 to 1
Outputs:
- vis_real: bfloat16 [512, 1024, 1024], P('freq', 'grp')
- vis_imag: bfloat16 [512, 1024, 1024], P('freq', 'grp')
The draws below stay inside these ranges and needn't reach their ends.
Inputs may be any that keep to these rules, and one draw needn't show every extreme that they name: `samples`: each word holds one signed 8-bit sample.
All inputs are finite; a program needn't handle non-finite values.
Results may differ from the reference program's by a relative error of at most 0.0065.
Values may be sent and summed in bfloat16 or wider, within the bound.
No kernel may reach another device: no remote copies, remote signals or barrier semaphores. Data moves between devices by JAX's collectives and lax.ppermute only.
A program may use at most 128 MiB of HBM per device.

```python
import math
import jax
import jax.numpy as jnp
from jax import lax

INPUTS = 1024
NFFT = 2048
CHAN = 512
TAPS = 4
SPEC = 128
SAMPLES = 268288
N_FREQ = 32


def with_ends(array, own_key, least, high):
    shape = array.shape
    place = [jax.random.randint(jax.random.fold_in(own_key, axis), (), 0, shape[axis]) for axis in range(len(shape))]
    array = array.at[tuple(place)].set(least)
    longest = shape.index(max(shape))
    place[longest] = (place[longest] + 1) % shape[longest]
    return array.at[tuple(place)].set(high)


def setup_inputs(seed: int = 0) -> dict:
    key_list = jax.random.split(jax.random.key(seed), 3)
    return {
        "samples": with_ends(jax.random.randint(key_list[0], (INPUTS, SAMPLES), -128, 128), jax.random.fold_in(key_list[0], 1), -128, 127).astype(jnp.int32),
        "window": jnp.clip(jax.random.uniform(key_list[1], (TAPS, NFFT), jnp.float32, 0.2, 1.0), 0.2, 1.0),
    }


def dft_table(fft_len, chan_count):
    rows_idx = jnp.arange(fft_len, dtype=jnp.int32)
    cols_idx = jnp.arange(chan_count, dtype=jnp.int32)
    phase_idx = rows_idx[:, None] * cols_idx[None, :] % fft_len
    angles = phase_idx.astype(jnp.float32) * (2.0 * math.pi / fft_len)
    stacked = jnp.stack([jnp.cos(angles), -jnp.sin(angles)], axis=2)
    return stacked.reshape(fft_len, 2 * chan_count).astype(jnp.bfloat16)

def reference(samples, window):
    cosines = dft_table(NFFT, CHAN).astype(jnp.float32)

    def spectra_of(in_block):
        rows_here = in_block.shape[0]
        voltage = in_block.astype(jnp.float32).reshape(rows_here, SPEC + TAPS - 1, NFFT) * (1.0 / 64.0)
        filtered = window[0] * voltage[:, 0:SPEC, :]
        for tap_idx in range(1, TAPS):
            filtered = filtered + window[tap_idx] * voltage[:, tap_idx:tap_idx + SPEC, :]
        filtered = filtered.astype(jnp.bfloat16).astype(jnp.float32)
        raw_sum = jnp.einsum('isj,jm->ims', filtered, cosines)
        raw_sum = raw_sum * (1.0 / math.sqrt(NFFT))
        return raw_sum.reshape(rows_here, CHAN, 2 * SPEC).astype(jnp.bfloat16)
    blocks_in = samples.reshape(INPUTS // 32, 32, samples.shape[1])
    spectra = lax.map(spectra_of, blocks_in).reshape(INPUTS, CHAN, 2 * SPEC)
    chan_dev = CHAN // N_FREQ
    by_block = jnp.moveaxis(spectra.reshape(INPUTS, N_FREQ, chan_dev, 2 * SPEC), 1, 0)

    def correlate(chan_block):
        values = chan_block.astype(jnp.float32)
        rotated = jnp.concatenate([values[..., SPEC:], -values[..., :SPEC]], axis=-1)
        real_part = jnp.einsum('ack,bck->cab', values, values) * (1.0 / SPEC)
        imag_part = jnp.einsum('ack,bck->cab', rotated, values) * (1.0 / SPEC)
        return (real_part.astype(jnp.bfloat16), imag_part.astype(jnp.bfloat16))
    vis_real, vis_imag = lax.map(correlate, by_block)
    return (vis_real.reshape(CHAN, INPUTS, INPUTS), vis_imag.reshape(CHAN, INPUTS, INPUTS))
```

```python
import math

import jax
import jax.numpy as jnp
import ml_dtypes
import numpy as np
from jax import lax
from jax.experimental import pallas as pl
from jax.experimental.pallas import tpu as pltpu
from jax.sharding import Mesh, PartitionSpec as P

CHAN = 512
NFFT = 2048
TAPS = 4
SPEC = 128
FRAMES = SPEC + TAPS - 1
ROWS_IN = 4
GROUPS = 8
N_FREQ = 32
CH = CHAN // N_FREQ
LANES = 128
SUB = 8
STEPS = 8
TILES = NFFT // LANES // STEPS
F32 = jnp.float32
BF16 = jnp.bfloat16
NT = (((1,), (1,)), ((), ()))


def table_rows():
    j = np.arange(NFFT, dtype=np.int64)
    c = np.arange(CHAN, dtype=np.int64)
    angle = ((c[:, None] * j[None, :]) % NFFT).astype(np.float32) * np.float32(2.0 * math.pi / NFFT)
    both = np.stack([np.cos(angle), -np.sin(angle)], axis=0)
    both = both.reshape(2, N_FREQ, CH, NFFT).transpose(1, 0, 2, 3)
    return both.reshape(2 * CHAN, NFFT).astype(ml_dtypes.bfloat16)


def channelize_kernel(s_ref, w_ref, t_ref, o_ref, f_ref):
    g = pl.program_id(0)
    per = TILES * ROWS_IN
    flat = s_ref.reshape(FRAMES * per, LANES)
    groups = SPEC // SUB
    for jt in range(TILES):
        cols = slice(jt * LANES, (jt + 1) * LANES)
        taps = [jnp.broadcast_to(w_ref[t : t + 1, cols] * (1.0 / 64.0), (SUB, LANES)) for t in range(TAPS)]
        for i in range(ROWS_IN):
            v = [
                flat[pl.ds(r * per + jt * ROWS_IN + i, SUB, stride=groups * per), :].astype(F32)
                for r in range(groups + TAPS - 1)
            ]
            rows = []
            for r in range(groups):
                acc = taps[0] * v[r]
                for t in range(1, TAPS):
                    acc = acc + taps[t] * v[r + t]
                rows.append(acc)
            block = jnp.concatenate(rows, axis=0).astype(BF16)
            f_ref[i * SPEC : (i + 1) * SPEC, pl.ds(pl.multiple_of((g * TILES + jt) * LANES, LANES), LANES)] = block

    @pl.when(g == STEPS - 1)
    def _():
        per_dev = 2 * CH
        tile = 256
        for mt in range(2 * CHAN // tile):
            raw = lax.dot_general(t_ref[mt * tile : (mt + 1) * tile, :], f_ref[...], NT, preferred_element_type=F32)
            out = (raw * (1.0 / math.sqrt(NFFT))).astype(BF16)
            for d in range(tile // per_dev):
                for i in range(ROWS_IN):
                    o_ref[mt * (tile // per_dev) + d, i] = out[d * per_dev : (d + 1) * per_dev, i * SPEC : (i + 1) * SPEC]


def channelize(samples, window, table):
    view = samples.reshape(ROWS_IN, FRAMES, NFFT // LANES, LANES).transpose(1, 2, 0, 3)
    view = view.reshape(FRAMES, NFFT // LANES * ROWS_IN, LANES)
    return pl.pallas_call(
        channelize_kernel,
        out_shape=jax.ShapeDtypeStruct((N_FREQ, ROWS_IN, 2 * CH, SPEC), BF16),
        grid=(STEPS,),
        in_specs=[
            pl.BlockSpec((FRAMES, TILES * ROWS_IN, LANES), lambda g: (0, g, 0)),
            pl.BlockSpec((TAPS, TILES * LANES), lambda g: (0, g)),
            pl.BlockSpec((2 * CHAN, NFFT), lambda g: (0, 0)),
        ],
        out_specs=pl.BlockSpec((N_FREQ, ROWS_IN, 2 * CH, SPEC), lambda g: (0, 0, 0, 0)),
        scratch_shapes=[pltpu.VMEM((ROWS_IN * SPEC, NFFT), BF16)],
        compiler_params=pltpu.CompilerParams(vmem_limit_bytes=40 << 20),
        cost_estimate=pl.CostEstimate(flops=2 * 512 * 2048 * 1024, bytes_accessed=9 << 20, transcendentals=0),
        name="channelize",
    )(view, window, table)


PARTS = ((0, 10), (10, 13), (13, 16))


def assemble_kernel(x_ref, *refs):
    outs, wide = refs[:-1], refs[-1]
    per = 2 * CH
    wide[...] = x_ref[...].reshape(SPEC * per, SPEC).astype(F32)
    for out, (lo, hi) in zip(outs, PARTS):
        for c in range(lo, hi):
            for p in range(2):
                out[c - lo, :, p * SPEC : (p + 1) * SPEC] = wide[pl.ds(p * CH + c, SPEC, stride=per), :].astype(BF16)


def assemble(x):
    return pl.pallas_call(
        assemble_kernel,
        out_shape=[jax.ShapeDtypeStruct((hi - lo, SPEC, 2 * SPEC), BF16) for lo, hi in PARTS],
        scratch_shapes=[pltpu.VMEM((SPEC * 2 * CH, SPEC), F32)],
        compiler_params=pltpu.CompilerParams(vmem_limit_bytes=40 << 20),
        cost_estimate=pl.CostEstimate(flops=0, bytes_accessed=2 << 20, transcendentals=0),
        name="assemble",
    )(x)


def correlate_kernel(col_ref, *refs):
    blocks, (re_ref, im_ref) = refs[:GROUPS], refs[-2:]
    own = blocks[0][0]
    rotated = jnp.concatenate([own[:, SPEC:], -own[:, :SPEC]], axis=1)
    left = jnp.concatenate([own, rotated], axis=0)
    for b in range(GROUPS):
        prod = lax.dot_general(left, blocks[b][0], NT, preferred_element_type=F32) * (1.0 / SPEC)
        cols = pl.ds(pl.multiple_of(col_ref[b], SPEC), SPEC)
        re_ref[0, :, cols] = prod[:SPEC].astype(BF16)
        im_ref[0, :, cols] = prod[SPEC:].astype(BF16)


def correlate(cols, blocks, lo, earlier):
    count, width = blocks[0].shape[0], SPEC * GROUPS
    shape = jax.ShapeDtypeStruct((CH, SPEC, width), BF16)
    in_specs = [pl.BlockSpec((1, SPEC, 2 * SPEC), lambda c, s: (c, 0, 0)) for _ in blocks]
    operands = list(blocks)
    aliases = {}
    if earlier is not None:
        in_specs += [pl.BlockSpec(memory_space=pl.ANY)] * 2
        operands += list(earlier)
        aliases = {1 + GROUPS: 0, 2 + GROUPS: 1}
    return pl.pallas_call(
        correlate_kernel,
        out_shape=[shape, shape],
        grid_spec=pltpu.PrefetchScalarGridSpec(
            num_scalar_prefetch=1,
            grid=(count,),
            in_specs=in_specs,
            out_specs=[pl.BlockSpec((1, SPEC, width), lambda c, s: (c + lo, 0, 0))] * 2,
        ),
        input_output_aliases=aliases,
        compiler_params=pltpu.CompilerParams(vmem_limit_bytes=40 << 20),
        cost_estimate=pl.CostEstimate(flops=count * 2 * 256 * 256 * 1024, bytes_accessed=count << 20, transcendentals=0),
        name="correlate",
    )(cols, *operands)


def shift(v, axis, size, by):
    return lax.ppermute(v, axis, [(i, (i + by) % size) for i in range(size)])


def gather(own, c_one, c_two):
    east = lambda v: shift(v, "x", 4, 1)
    west = lambda v: shift(v, "x", 4, -1)
    across = lambda v: shift(v, "z_lo", 2, 1)
    z = across(own)
    one_w, two_w, one_e, two_e = east(c_one), east(c_two), west(c_one), west(c_two)
    own_w, own_e = east(own), west(own)
    z_w, z_e = east(z), west(z)
    one_o, two_o = east(one_w), west(two_e)
    own_o, z_o = east(own_w), west(z_e)
    main = (own, z, own_e, z_e, own_o, z_o, own_w, z_w)
    first = (c_one, one_e, one_o, one_w)
    second = (c_two, two_e, two_o, two_w)
    first = [b for v in first for b in (v, across(v))]
    second = [b for v in second for b in (v, across(v))]
    return main, first, second


def on_device(samples, window):
    table = jnp.asarray(table_rows())
    pieces = channelize(samples, window, table)
    arrived = lax.all_to_all(pieces, ("y", "z_hi", "core"), split_axis=0, concat_axis=0, tiled=True)
    parts = assemble(arrived.reshape(SPEC, 2 * CH, SPEC))
    gathered = gather(*parts)
    x, z = lax.axis_index("x"), lax.axis_index("z_lo")
    cols = jnp.stack([((x + dx) % 4 * 2 + (z + dz) % 2) * SPEC for dx in range(4) for dz in range(2)]).astype(jnp.int32)
    out = None
    for blocks, (lo, _) in reversed(list(zip(gathered, PARTS))):
        out = correlate(cols, blocks, lo, out)
    return tuple(out)


def solution(mesh):
    axes = ("x", "z_lo", "y", "z_hi", "core")
    fine = Mesh(mesh.devices.reshape(4, 2, 4, 4, 2), axes)
    return jax.shard_map(
        on_device,
        mesh=fine,
        in_specs=(P(axes, None), P()),
        out_specs=(P(axes[2:], axes[:2], None), P(axes[2:], axes[:2], None)),
        check_vma=False,
    )
```

```python
import math

import jax
import jax.numpy as jnp
import ml_dtypes
import numpy as np
from jax import lax
from jax.experimental import pallas as pl
from jax.experimental.pallas import tpu as pltpu
from jax.sharding import Mesh, PartitionSpec as P

CHAN = 512
NFFT = 2048
TAPS = 4
SPEC = 128
FRAMES = SPEC + TAPS - 1
ROWS_IN = 4
GROUPS = 8
N_FREQ = 32
CH = CHAN // N_FREQ
LANES = 128
SUB = 8
F32 = jnp.float32
BF16 = jnp.bfloat16
NT = (((1,), (1,)), ((), ()))
MIB = 1 << 20
FREQ = ("y", "z_hi", "core")

CHUNKS = ((6, 2), (5, 3))
STARTS = (0, 8)


def table_rows(lo, count):
    j = np.arange(NFFT, dtype=np.int64)
    c = (np.arange(N_FREQ)[:, None] * CH + lo + np.arange(count)[None, :]).reshape(-1)
    angle = ((c[:, None] * j[None, :]) % NFFT).astype(np.float32) * np.float32(2.0 * math.pi / NFFT)
    both = np.stack([np.cos(angle), -np.sin(angle)], axis=0)
    both = both.reshape(2, N_FREQ, count, NFFT).transpose(1, 0, 2, 3)
    return jnp.asarray(both.reshape(2 * N_FREQ * count, NFFT).astype(ml_dtypes.bfloat16))


def store_spectra(raw, o_ref, first, per):
    out = (raw * (1.0 / math.sqrt(NFFT))).astype(BF16)
    for d in range(raw.shape[0] // per):
        for i in range(ROWS_IN):
            o_ref[first + d, i] = out[d * per : (d + 1) * per, i * SPEC : (i + 1) * SPEC]


def filter_kernel(rows, s_hbm, w_ref, t_hbm, o_ref, f_hbm, s_ref, t_ref, f_ref, wv_ref, s_sem, t_sem, f_sem):
    parts = 4
    span = SPEC // parts
    edges = [0] + [(h + 1) * span + TAPS - 1 for h in range(parts)]
    arrivals = []
    for h in range(parts):
        cut = pl.ds(edges[h], edges[h + 1] - edges[h])
        arrivals.append(pltpu.make_async_copy(s_hbm.at[cut], s_ref.at[cut], s_sem.at[h]))
    for copy in arrivals:
        copy.start()
    table_copy = pltpu.make_async_copy(t_hbm, t_ref, t_sem)
    table_copy.start()
    pairs = NFFT // LANES // 2
    for a in range(pairs):
        for t in range(TAPS):
            halves = [
                jnp.broadcast_to(w_ref[t : t + 1, (2 * a + b) * LANES : (2 * a + b + 1) * LANES] * (1.0 / 64.0), (ROWS_IN, LANES))
                for b in range(2)
            ]
            wv_ref[a, t] = jnp.concatenate(halves, axis=0)
    for h in range(parts):
        arrivals[h].wait()

        def step(a, carry):
            sub = pl.ds(pl.multiple_of(a * SUB, SUB), SUB)
            taps = [wv_ref[a, t] for t in range(TAPS)]
            for s0 in range(h * span, (h + 1) * span, 2 * SUB):
                v = [s_ref[s0 + k, sub, :].astype(F32) for k in range(2 * SUB + TAPS - 1)]
                sums = []
                for k in range(2 * SUB):
                    acc = taps[0] * v[k]
                    for t in range(1, TAPS):
                        acc = acc + taps[t] * v[k + t]
                    sums.append(acc)
                low = jnp.swapaxes(jnp.stack(sums[:SUB], axis=0), 0, 1)
                high = jnp.swapaxes(jnp.stack(sums[SUB:], axis=0), 0, 1)
                both = jnp.concatenate([low, high], axis=1).astype(BF16)
                for b in range(2):
                    lane = pl.ds(pl.multiple_of((2 * a + b) * LANES, LANES), LANES)
                    for i in range(ROWS_IN):
                        f_ref[i * SPEC + s0 : i * SPEC + s0 + 2 * SUB, lane] = both[b * ROWS_IN + i]
            return carry

        lax.fori_loop(0, pairs, step, 0)
    out_copy = pltpu.make_async_copy(f_ref, f_hbm, f_sem)
    out_copy.start()
    table_copy.wait()
    tile = 256
    per = rows // N_FREQ
    for m in range(rows // tile):
        raw = lax.dot_general(t_ref[m * tile : (m + 1) * tile, :], f_ref[...], NT, preferred_element_type=F32)
        store_spectra(raw, o_ref, m * (tile // per), per)
    out_copy.wait()


def filter_and_transform(samples, window, table):
    view = samples.reshape(ROWS_IN, FRAMES, NFFT // LANES, LANES).transpose(1, 2, 0, 3)
    view = view.reshape(FRAMES, NFFT // LANES * ROWS_IN, LANES)
    rows = table.shape[0]
    return pl.pallas_call(
        lambda *refs: filter_kernel(rows, *refs),
        out_shape=[
            jax.ShapeDtypeStruct((N_FREQ, ROWS_IN, rows // N_FREQ, SPEC), BF16),
            jax.ShapeDtypeStruct((ROWS_IN * SPEC, NFFT), BF16),
        ],
        in_specs=[
            pl.BlockSpec(memory_space=pl.ANY),
            pl.BlockSpec(memory_space=pltpu.VMEM),
            pl.BlockSpec(memory_space=pl.ANY),
        ],
        out_specs=[pl.BlockSpec(memory_space=pltpu.VMEM), pl.BlockSpec(memory_space=pl.ANY)],
        scratch_shapes=[
            pltpu.VMEM((FRAMES, NFFT // LANES * ROWS_IN, LANES), jnp.int32),
            pltpu.VMEM((rows, NFFT), BF16),
            pltpu.VMEM((ROWS_IN * SPEC, NFFT), BF16),
            pltpu.VMEM((NFFT // LANES // 2, TAPS, SUB, LANES), F32),
            pltpu.SemaphoreType.DMA((4,)),
            pltpu.SemaphoreType.DMA,
            pltpu.SemaphoreType.DMA,
        ],
        compiler_params=pltpu.CompilerParams(vmem_limit_bytes=60 * MIB),
        cost_estimate=pl.CostEstimate(flops=2 * rows * 512 * 2048, bytes_accessed=9 * MIB, transcendentals=0),
        name="filter_and_transform",
    )(view, window, table)


def transform_kernel(per, f_ref, t_ref, o_ref):
    raw = lax.dot_general(t_ref[...], f_ref[...], NT, preferred_element_type=F32)
    store_spectra(raw, o_ref, 0, per)


def transform(filtered, table):
    rows, tile = table.shape[0], 256
    per = rows // N_FREQ
    return pl.pallas_call(
        lambda *refs: transform_kernel(per, *refs),
        out_shape=jax.ShapeDtypeStruct((N_FREQ, ROWS_IN, per, SPEC), BF16),
        grid=(rows // tile,),
        in_specs=[pl.BlockSpec((ROWS_IN * SPEC, NFFT), lambda g: (0, 0)), pl.BlockSpec((tile, NFFT), lambda g: (g, 0))],
        out_specs=pl.BlockSpec((tile // per, ROWS_IN, per, SPEC), lambda g: (g, 0, 0, 0)),
        compiler_params=pltpu.CompilerParams(vmem_limit_bytes=12 * MIB),
        cost_estimate=pl.CostEstimate(flops=2 * rows * 512 * 2048, bytes_accessed=5 * MIB, transcendentals=0),
        name="transform",
    )(filtered, table)


def assemble_kernel(sizes, x_ref, *refs):
    outs, wide = refs[:-1], refs[-1]
    count = sum(sizes)
    wide[...] = x_ref[...].reshape(SPEC * 2 * count, SPEC).astype(F32)
    lo = 0
    for out, size in zip(outs, sizes):
        for c in range(size):
            for p in range(2):
                rows = pl.ds(p * count + lo + c, SPEC, stride=2 * count)
                out[c, :, p * SPEC : (p + 1) * SPEC] = wide[rows, :].astype(BF16)
        lo += size


def assemble(pieces, sizes):
    count = sum(sizes)
    return pl.pallas_call(
        lambda *refs: assemble_kernel(sizes, *refs),
        out_shape=[jax.ShapeDtypeStruct((size, SPEC, 2 * SPEC), BF16) for size in sizes],
        scratch_shapes=[pltpu.VMEM((SPEC * 2 * count, SPEC), F32)],
        compiler_params=pltpu.CompilerParams(vmem_limit_bytes=6 * MIB),
        cost_estimate=pl.CostEstimate(flops=0, bytes_accessed=2 * MIB, transcendentals=0),
        name="assemble",
    )(pieces.reshape(SPEC, 2 * count, SPEC))


def correlate_kernel(col_ref, *refs):
    blocks, (re_ref, im_ref) = refs[:GROUPS], refs[-2:]
    c = pl.program_id(0)
    own = blocks[0][c]
    rotated = jnp.concatenate([own[:, SPEC:], -own[:, :SPEC]], axis=1)
    left = jnp.concatenate([own, rotated], axis=0)
    for b in range(0, GROUPS, 2):
        right = jnp.concatenate([blocks[b][c], blocks[b + 1][c]], axis=0)
        prod = lax.dot_general(left, right, NT, preferred_element_type=F32) * (1.0 / SPEC)
        for h in range(2):
            cols = pl.ds(pl.multiple_of(col_ref[b + h], SPEC), SPEC)
            re_ref[0, :, cols] = prod[:SPEC, h * SPEC : (h + 1) * SPEC].astype(BF16)
            im_ref[0, :, cols] = prod[SPEC:, h * SPEC : (h + 1) * SPEC].astype(BF16)


def correlate(cols, blocks, lo, earlier):
    count, width = blocks[0].shape[0], SPEC * GROUPS
    shape = jax.ShapeDtypeStruct((CH, SPEC, width), BF16)
    in_specs = [pl.BlockSpec(memory_space=pltpu.VMEM) for _ in blocks]
    operands = list(blocks)
    aliases = {}
    if earlier is not None:
        in_specs += [pl.BlockSpec(memory_space=pl.ANY)] * 2
        operands += list(earlier)
        aliases = {1 + GROUPS: 0, 2 + GROUPS: 1}
    return pl.pallas_call(
        correlate_kernel,
        out_shape=[shape, shape],
        grid_spec=pltpu.PrefetchScalarGridSpec(
            num_scalar_prefetch=1,
            grid=(count,),
            in_specs=in_specs,
            out_specs=[pl.BlockSpec((1, SPEC, width), lambda c, s: (c + lo, 0, 0))] * 2,
        ),
        input_output_aliases=aliases,
        compiler_params=pltpu.CompilerParams(vmem_limit_bytes=8 * MIB),
        cost_estimate=pl.CostEstimate(flops=count * 2 * 256 * 256 * 1024, bytes_accessed=count * MIB, transcendentals=0),
        name="correlate",
    )(cols, *operands)


class Queue:
    def __init__(self, axis, size, by, depth):
        self.axis, self.pairs, self.depth = axis, [(i, (i + by) % size) for i in range(size)], depth
        self.ended = []

    def send(self, value):
        if len(self.ended) >= self.depth:
            value, _ = lax.optimization_barrier((value, self.ended[-self.depth]))
        self.ended.append(lax.ppermute(value, self.axis, self.pairs))
        return self.ended[-1]


def exchange(pieces):
    return lax.all_to_all(pieces, FREQ, split_axis=0, concat_axis=0, tiled=True)


def on_device(samples, window):
    tables = [table_rows(lo, sum(sizes)) for lo, sizes in zip(STARTS, CHUNKS)]
    x, z = lax.axis_index("x"), lax.axis_index("z_lo")
    cols = jnp.stack([((x + dx) % 4 * 2 + (z + dz) % 2) * SPEC for dx in range(4) for dz in range(2)]).astype(jnp.int32)
    up, down, across = Queue("x", 4, 1, 2), Queue("x", 4, -1, 2), Queue("z_lo", 2, 1, 1)

    pieces, filtered = filter_and_transform(samples, window, tables[0])
    arrived = exchange(pieces)
    main, late = assemble(arrived, CHUNKS[0])
    filtered, _ = lax.optimization_barrier((filtered, main))
    arrived = exchange(transform(filtered, tables[1]))

    def gather(main, late, late_first):
        z_main = across.send(main)
        if late_first:
            late_m, late_p = up.send(late), down.send(late)
        main_m, main_p = up.send(main), down.send(main)
        if not late_first:
            late_m, late_p = up.send(late), down.send(late)
            late_o = None
        else:
            late_o = down.send(late_p)
        z_late = across.send(late)
        z_m, z_p = up.send(z_main), down.send(z_main)
        z_late_m, z_late_p = across.send(late_m), across.send(late_p)
        main_o, z_o = up.send(main_m), down.send(z_p)
        if late_o is None:
            late_o = up.send(late_m)
        z_late_o = across.send(late_o)
        return (
            (main, z_main, main_p, z_p, main_o, z_o, main_m, z_m),
            (late, z_late, late_p, z_late_p, late_o, z_late_o, late_m, z_late_m),
        )

    first = gather(main, late, False)
    main, late = assemble(arrived, CHUNKS[1])
    second = gather(main, late, True)
    out = None
    for blocks, lo, sizes in ((first, STARTS[0], CHUNKS[0]), (second, STARTS[1], CHUNKS[1])):
        out = correlate(cols, blocks[0], lo, out)
        out = correlate(cols, blocks[1], lo + sizes[0], out)
    return tuple(out)


def solution(mesh):
    axes = ("x", "z_lo") + FREQ
    fine = Mesh(mesh.devices.reshape(4, 2, 4, 4, 2), axes)
    return jax.shard_map(
        on_device,
        mesh=fine,
        in_specs=(P(axes, None), P()),
        out_specs=(P(FREQ, axes[:2], None), P(FREQ, axes[:2], None)),
        check_vma=False,
    )
```

```python
import math

import jax
import jax.numpy as jnp
import ml_dtypes
import numpy as np
from jax import lax
from jax.experimental import pallas as pl
from jax.experimental.pallas import tpu as pltpu
from jax.sharding import Mesh, PartitionSpec as P

CHAN = 512
NFFT = 2048
TAPS = 4
SPEC = 128
FRAMES = SPEC + TAPS - 1
ROWS_IN = 4
GROUPS = 8
N_FREQ = 32
CH = CHAN // N_FREQ
LANES = 128
SUB = 8
F32 = jnp.float32
BF16 = jnp.bfloat16
NT = (((1,), (1,)), ((), ()))
MIB = 1 << 20
FREQ = ("y", "z_hi", "core")
LIGHT = pl.CostEstimate(flops=1000, bytes_accessed=1000, transcendentals=0)

EARLY = 8


def table_rows(lo, count):
    j = np.arange(NFFT, dtype=np.int64)
    c = (np.arange(N_FREQ)[:, None] * CH + lo + np.arange(count)[None, :]).reshape(-1)
    angle = ((c[:, None] * j[None, :]) % NFFT).astype(np.float32) * np.float32(2.0 * math.pi / NFFT)
    both = np.stack([np.cos(angle), -np.sin(angle)], axis=0)
    both = both.reshape(2, N_FREQ, count, NFFT).transpose(1, 0, 2, 3)
    return jnp.asarray(both.reshape(2 * N_FREQ * count, NFFT).astype(ml_dtypes.bfloat16))


def store_spectra(raw, o_ref, first, per):
    out = (raw * (1.0 / math.sqrt(NFFT))).astype(BF16)
    for d in range(raw.shape[0] // per):
        for i in range(ROWS_IN):
            o_ref[first + d, i] = out[d * per : (d + 1) * per, i * SPEC : (i + 1) * SPEC]


def filter_kernel(rows, s_hbm, w_ref, t_hbm, o_ref, s_ref, t_ref, f_ref, wv_ref, s_sem, t_sem):
    parts = 4
    span = SPEC // parts
    edges = [0] + [(h + 1) * span + TAPS - 1 for h in range(parts)]
    arrivals = []
    for h in range(parts):
        cut = pl.ds(edges[h], edges[h + 1] - edges[h])
        arrivals.append(pltpu.make_async_copy(s_hbm.at[cut], s_ref.at[cut], s_sem.at[h]))
    for copy in arrivals:
        copy.start()
    table_copy = pltpu.make_async_copy(t_hbm, t_ref, t_sem)
    table_copy.start()
    pairs = NFFT // LANES // 2
    for a in range(pairs):
        for t in range(TAPS):
            halves = [
                jnp.broadcast_to(w_ref[t : t + 1, (2 * a + b) * LANES : (2 * a + b + 1) * LANES] * (1.0 / 64.0), (ROWS_IN, LANES))
                for b in range(2)
            ]
            wv_ref[a, t] = jnp.concatenate(halves, axis=0)
    for h in range(parts):
        arrivals[h].wait()

        def step(a, carry):
            sub = pl.ds(pl.multiple_of(a * SUB, SUB), SUB)
            taps = [wv_ref[a, t] for t in range(TAPS)]
            for s0 in range(h * span, (h + 1) * span, 2 * SUB):
                v = [s_ref[s0 + k, sub, :].astype(F32) for k in range(2 * SUB + TAPS - 1)]
                sums = []
                for k in range(2 * SUB):
                    acc = taps[0] * v[k]
                    for t in range(1, TAPS):
                        acc = acc + taps[t] * v[k + t]
                    sums.append(acc)
                low = jnp.swapaxes(jnp.stack(sums[:SUB], axis=0), 0, 1)
                high = jnp.swapaxes(jnp.stack(sums[SUB:], axis=0), 0, 1)
                both = jnp.concatenate([low, high], axis=1).astype(BF16)
                for b in range(2):
                    lane = pl.ds(pl.multiple_of((2 * a + b) * LANES, LANES), LANES)
                    for i in range(ROWS_IN):
                        f_ref[i * SPEC + s0 : i * SPEC + s0 + 2 * SUB, lane] = both[b * ROWS_IN + i]
            return carry

        lax.fori_loop(0, pairs, step, 0)
    table_copy.wait()
    tile = 256
    per = rows // N_FREQ
    for m in range(rows // tile):
        raw = lax.dot_general(t_ref[m * tile : (m + 1) * tile, :], f_ref[...], NT, preferred_element_type=F32)
        store_spectra(raw, o_ref, m * (tile // per), per)


def filter_and_transform(samples, window, table):
    view = samples.reshape(ROWS_IN, FRAMES, NFFT // LANES, LANES).transpose(1, 2, 0, 3)
    view = view.reshape(FRAMES, NFFT // LANES * ROWS_IN, LANES)
    rows = table.shape[0]
    return pl.pallas_call(
        lambda *refs: filter_kernel(rows, *refs),
        out_shape=jax.ShapeDtypeStruct((N_FREQ, ROWS_IN, rows // N_FREQ, SPEC), BF16),
        in_specs=[
            pl.BlockSpec(memory_space=pl.ANY),
            pl.BlockSpec(memory_space=pltpu.VMEM),
            pl.BlockSpec(memory_space=pl.ANY),
        ],
        out_specs=pl.BlockSpec(memory_space=pltpu.VMEM),
        scratch_shapes=[
            pltpu.VMEM((FRAMES, NFFT // LANES * ROWS_IN, LANES), jnp.int32),
            pltpu.VMEM((rows, NFFT), BF16),
            pltpu.VMEM((ROWS_IN * SPEC, NFFT), BF16),
            pltpu.VMEM((NFFT // LANES // 2, TAPS, SUB, LANES), F32),
            pltpu.SemaphoreType.DMA((4,)),
            pltpu.SemaphoreType.DMA,
        ],
        compiler_params=pltpu.CompilerParams(vmem_limit_bytes=60 * MIB),
        cost_estimate=LIGHT,
        name="filter_and_transform",
    )(view, window, table)


def assemble_kernel(sizes, x_ref, *refs):
    outs, wide = refs[:-1], refs[-1]
    count, pitch = sum(sizes), wide.shape[1]
    wide[:, : 2 * count, :] = x_ref[...].astype(F32)
    flat = wide.reshape(SPEC * pitch, SPEC)
    lo = 0
    for out, size in zip(outs, sizes):
        for c in range(size):
            for p in range(2):
                rows = pl.ds(p * count + lo + c, SPEC, stride=pitch)
                out[c, :, p * SPEC : (p + 1) * SPEC] = flat[rows, :].astype(BF16)
        lo += size


def assemble(pieces, sizes):
    count = sum(sizes)
    pitch = 2 * count + SUB if 2 * count // SUB % 2 == 0 else 2 * count
    return pl.pallas_call(
        lambda *refs: assemble_kernel(sizes, *refs),
        out_shape=[jax.ShapeDtypeStruct((size, SPEC, 2 * SPEC), BF16) for size in sizes],
        scratch_shapes=[pltpu.VMEM((SPEC, pitch, SPEC), F32)],
        compiler_params=pltpu.CompilerParams(vmem_limit_bytes=8 * MIB),
        cost_estimate=LIGHT,
        name="assemble",
    )(pieces.reshape(SPEC, 2 * count, SPEC))


def products(own, other):
    rotated = jnp.concatenate([own[:, SPEC:], -own[:, :SPEC]], axis=1)
    left = jnp.concatenate([own, rotated], axis=0)
    return (lax.dot_general(left, other, NT, preferred_element_type=F32) * (1.0 / SPEC)).astype(BF16)


def correlate_kernel(plan, last, place_ref, *refs):
    count = 1 + max(k for part in plan for k in (part[1],) + tuple(b for b, _ in part[2]))
    blocks, refs = refs[:count], refs[count:]
    if last:
        re_ref, im_ref = refs[:2]
        re_out, im_out, sem = refs[-3:]
    else:
        re_ref, im_ref = refs[-2:]
    copies = []
    for lo, own, others in plan:
        size = blocks[own].shape[0]

        def one(c):
            for k in range(0, len(others), 2):
                pair = others[k : k + 2]
                right = jnp.concatenate([blocks[b][c] for b, _ in pair], axis=0)
                out = products(blocks[own][c], right)
                for h, (_, spot) in enumerate(pair):
                    cols = pl.ds(pl.multiple_of(place_ref[spot], SPEC), SPEC)
                    re_ref[lo + c, :, cols] = out[:SPEC, h * SPEC : (h + 1) * SPEC]
                    im_ref[lo + c, :, cols] = out[SPEC:, h * SPEC : (h + 1) * SPEC]

        if last:
            for c in range(size):
                one(c)
                for k, (src, dst) in enumerate(((re_ref, re_out), (im_ref, im_out))):
                    copies.append(pltpu.make_async_copy(src.at[lo + c], dst.at[lo + c], sem.at[k, lo + c]))
                    copies[-1].start()
        else:
            lax.fori_loop(0, size, lambda c, carry: (one(c), carry)[1], 0, unroll=4)
    for copy in copies:
        copy.wait()


def correlate(place, plan, blocks, so_far=None, last=False, earlier=None):
    shape = jax.ShapeDtypeStruct((CH, SPEC, SPEC * GROUPS), BF16)
    vmem = pl.BlockSpec(memory_space=pltpu.VMEM)
    operands = [place] + list(blocks) + list(so_far or ())
    in_specs = [pl.BlockSpec(memory_space=pltpu.SMEM)] + [vmem] * (len(operands) - 1)
    aliases, scratch, out_specs = {}, [], [vmem] * 2
    if last:
        out_specs = [pl.BlockSpec(memory_space=pl.ANY)] * 2
        scratch = [pltpu.SemaphoreType.DMA((2, CH))]
        if earlier is not None:
            aliases = {len(operands): 0, len(operands) + 1: 1}
            operands += list(earlier)
            in_specs += out_specs
    elif so_far is not None:
        aliases = {1 + len(blocks): 0, 2 + len(blocks): 1}
    return pl.pallas_call(
        lambda *refs: correlate_kernel(plan, last, *refs),
        out_shape=[shape, shape],
        in_specs=in_specs,
        out_specs=out_specs,
        scratch_shapes=scratch,
        input_output_aliases=aliases,
        compiler_params=pltpu.CompilerParams(vmem_limit_bytes=16 * MIB),
        cost_estimate=LIGHT,
        name="correlate",
    )(*operands)


def shift(value, axis, by):
    size = lax.axis_size(axis)
    return lax.ppermute(value, axis, [(i, (i + by) % size) for i in range(size)])


def up(value):
    return shift(value, "x", 1)


def down(value):
    return shift(value, "x", -1)


def across(value):
    return shift(value, "z_lo", 1)


def after(values, done):
    return lax.optimization_barrier((values, done))


def on_device(samples, window):
    x, z = lax.axis_index("x"), lax.axis_index("z_lo")
    place = jnp.stack([((x + dx) % 4 * 2 + (z + dz) % 2) * SPEC for dx in range(4) for dz in range(2)]).astype(jnp.int32)

    pieces = filter_and_transform(samples, window, table_rows(0, CH))
    arrived = lax.all_to_all(pieces, FREQ, split_axis=0, concat_axis=0, tiled=True)
    a, b = assemble(arrived, (EARLY, CH - EARLY))
    b_m, b_p, za = up(b), down(b), across(a)
    a_m, a_p, zb = up(a), down(a), across(b)
    (za, b_p, b_m), _ = after((za, b_p, b_m), (za, b_p, b_m))
    za_m, b_o, zb_m = up(za), down(b_p), across(b_m)
    a_o, za_p, zb_p = up(a_m), down(za), across(b_p)
    out = correlate(
        place,
        (
            (0, 0, ((0, 0), (2, 1), (3, 6), (4, 2))),
            (EARLY, 1, ((1, 0), (5, 1), (6, 6), (7, 2))),
        ),
        (a, b, za, a_m, a_p, zb, b_m, b_p),
    )
    (za_m, b_o), out = after((za_m, b_o), out)
    za_o, zb_o = up(za_m), across(b_o)
    out = correlate(
        place,
        (
            (0, 0, ((2, 7), (3, 3), (4, 4))),
            (EARLY, 1, ((5, 7), (6, 3), (7, 4))),
        ),
        (a, b, za_m, za_p, a_o, zb_m, zb_p, b_o),
        out,
    )
    done = correlate(place, ((0, 0, ((1, 5),)),), (a, za_o), out, last=True)
    done = correlate(place, ((EARLY, 0, ((1, 5),)),), (b, zb_o), out, last=True, earlier=done)
    return tuple(done)


def solution(mesh):
    axes = ("x", "z_lo") + FREQ
    fine = Mesh(mesh.devices.reshape(4, 2, 4, 4, 2), axes)
    return jax.shard_map(
        on_device,
        mesh=fine,
        in_specs=(P(axes, None), P()),
        out_specs=(P(FREQ, axes[:2], None), P(FREQ, axes[:2], None)),
        check_vma=False,
    )
```

```python
import math

import jax
import jax.numpy as jnp
import ml_dtypes
import numpy as np
from jax import lax
from jax.experimental import pallas as pl
from jax.experimental.pallas import tpu as pltpu
from jax.sharding import Mesh, PartitionSpec as P

CHAN = 512
NFFT = 2048
TAPS = 4
SPEC = 128
FRAMES = SPEC + TAPS - 1
ROWS_IN = 4
GROUPS = 8
N_FREQ = 32
CH = CHAN // N_FREQ
LANES = 128
SUB = 8
F32 = jnp.float32
BF16 = jnp.bfloat16
NT = (((1,), (1,)), ((), ()))
MIB = 1 << 20
FREQ = ("y", "z_hi", "core")
LIGHT = pl.CostEstimate(flops=1000, bytes_accessed=1000, transcendentals=0)

EARLY = 8


def table_rows(lo, count):
    j = np.arange(NFFT, dtype=np.int64)
    c = (np.arange(N_FREQ)[:, None] * CH + lo + np.arange(count)[None, :]).reshape(-1)
    angle = ((c[:, None] * j[None, :]) % NFFT).astype(np.float32) * np.float32(2.0 * math.pi / NFFT)
    both = np.stack([np.cos(angle), -np.sin(angle)], axis=0)
    both = both.reshape(2, N_FREQ, count, NFFT).transpose(1, 0, 2, 3)
    return jnp.asarray(both.reshape(2 * N_FREQ * count, NFFT).astype(ml_dtypes.bfloat16))


def store_spectra(raw, o_ref, first, per):
    out = (raw * (1.0 / math.sqrt(NFFT))).astype(BF16)
    for d in range(raw.shape[0] // per):
        for i in range(ROWS_IN):
            o_ref[first + d, i] = out[d * per : (d + 1) * per, i * SPEC : (i + 1) * SPEC]


def filter_kernel(rows, s_hbm, w_ref, t_hbm, o_ref, s_ref, t_ref, f_ref, wv_ref, s_sem, t_sem):
    parts = 4
    span = SPEC // parts
    edges = [0] + [(h + 1) * span + TAPS - 1 for h in range(parts)]
    arrivals = []
    for h in range(parts):
        cut = pl.ds(edges[h], edges[h + 1] - edges[h])
        arrivals.append(pltpu.make_async_copy(s_hbm.at[cut], s_ref.at[cut], s_sem.at[h]))
    for copy in arrivals:
        copy.start()
    table_copy = pltpu.make_async_copy(t_hbm, t_ref, t_sem)
    table_copy.start()
    pairs = NFFT // LANES // 2
    for a in range(pairs):
        for t in range(TAPS):
            halves = [
                jnp.broadcast_to(w_ref[t : t + 1, (2 * a + b) * LANES : (2 * a + b + 1) * LANES] * (1.0 / 64.0), (ROWS_IN, LANES))
                for b in range(2)
            ]
            wv_ref[a, t] = jnp.concatenate(halves, axis=0)
    for h in range(parts):
        arrivals[h].wait()

        def step(a, carry):
            sub = pl.ds(pl.multiple_of(a * SUB, SUB), SUB)
            taps = [wv_ref[a, t] for t in range(TAPS)]
            for s0 in range(h * span, (h + 1) * span, 2 * SUB):
                v = [s_ref[s0 + k, sub, :].astype(F32) for k in range(2 * SUB + TAPS - 1)]
                sums = []
                for k in range(2 * SUB):
                    acc = taps[0] * v[k]
                    for t in range(1, TAPS):
                        acc = acc + taps[t] * v[k + t]
                    sums.append(acc)
                low = jnp.swapaxes(jnp.stack(sums[:SUB], axis=0), 0, 1)
                high = jnp.swapaxes(jnp.stack(sums[SUB:], axis=0), 0, 1)
                both = jnp.concatenate([low, high], axis=1).astype(BF16)
                for b in range(2):
                    lane = pl.ds(pl.multiple_of((2 * a + b) * LANES, LANES), LANES)
                    for i in range(ROWS_IN):
                        f_ref[i * SPEC + s0 : i * SPEC + s0 + 2 * SUB, lane] = both[b * ROWS_IN + i]
            return carry

        lax.fori_loop(0, pairs, step, 0)
    table_copy.wait()
    tile = 256
    per = rows // N_FREQ
    for m in range(rows // tile):
        raw = lax.dot_general(t_ref[m * tile : (m + 1) * tile, :], f_ref[...], NT, preferred_element_type=F32)
        store_spectra(raw, o_ref, m * (tile // per), per)


def filter_and_transform(samples, window, table):
    view = samples.reshape(ROWS_IN, FRAMES, NFFT // LANES, LANES).transpose(1, 2, 0, 3)
    view = view.reshape(FRAMES, NFFT // LANES * ROWS_IN, LANES)
    rows = table.shape[0]
    return pl.pallas_call(
        lambda *refs: filter_kernel(rows, *refs),
        out_shape=jax.ShapeDtypeStruct((N_FREQ, ROWS_IN, rows // N_FREQ, SPEC), BF16),
        in_specs=[
            pl.BlockSpec(memory_space=pl.ANY),
            pl.BlockSpec(memory_space=pltpu.VMEM),
            pl.BlockSpec(memory_space=pl.ANY),
        ],
        out_specs=pl.BlockSpec(memory_space=pltpu.VMEM),
        scratch_shapes=[
            pltpu.VMEM((FRAMES, NFFT // LANES * ROWS_IN, LANES), jnp.int32),
            pltpu.VMEM((rows, NFFT), BF16),
            pltpu.VMEM((ROWS_IN * SPEC, NFFT), BF16),
            pltpu.VMEM((NFFT // LANES // 2, TAPS, SUB, LANES), F32),
            pltpu.SemaphoreType.DMA((4,)),
            pltpu.SemaphoreType.DMA,
        ],
        compiler_params=pltpu.CompilerParams(vmem_limit_bytes=60 * MIB),
        cost_estimate=LIGHT,
        name="filter_and_transform",
    )(view, window, table)


def assemble_kernel(sizes, x_ref, *refs):
    outs, wide = refs[:-1], refs[-1]
    count, pitch = sum(sizes), wide.shape[1]
    wide[:, : 2 * count, :] = x_ref[...].astype(F32)
    flat = wide.reshape(SPEC * pitch, SPEC)
    lo = 0
    for out, size in zip(outs, sizes):
        for c in range(size):
            for p in range(2):
                rows = pl.ds(p * count + lo + c, SPEC, stride=pitch)
                out[c, :, p * SPEC : (p + 1) * SPEC] = flat[rows, :].astype(BF16)
        lo += size


def assemble(pieces, sizes):
    count = sum(sizes)
    pitch = 2 * count + SUB if 2 * count // SUB % 2 == 0 else 2 * count
    return pl.pallas_call(
        lambda *refs: assemble_kernel(sizes, *refs),
        out_shape=[jax.ShapeDtypeStruct((size, SPEC, 2 * SPEC), BF16) for size in sizes],
        scratch_shapes=[pltpu.VMEM((SPEC, pitch, SPEC), F32)],
        compiler_params=pltpu.CompilerParams(vmem_limit_bytes=8 * MIB),
        cost_estimate=LIGHT,
        name="assemble",
    )(pieces.reshape(SPEC, 2 * count, SPEC))


def products(own, other):
    rotated = jnp.concatenate([own[:, SPEC:], -own[:, :SPEC]], axis=1)
    left = jnp.concatenate([own, rotated], axis=0)
    return (lax.dot_general(left, other, NT, preferred_element_type=F32) * (1.0 / SPEC)).astype(BF16)


def correlate_kernel(plan, count, place_ref, *refs):
    blocks, refs = refs[:count], refs[count:]
    copies = []
    if len(refs) == 2:
        re_ref, im_ref = refs
    else:
        re_ref, im_ref, re_out, im_out, sem = refs[-5:]
    for lo, own, others in plan:

        def one(c, carry):
            for k in range(0, len(others), 2):
                pair = others[k : k + 2]
                right = jnp.concatenate([blocks[b][c] for b, _ in pair], axis=0)
                out = products(blocks[own][c], right)
                for h, (_, spot) in enumerate(pair):
                    cols = pl.ds(pl.multiple_of(place_ref[spot], SPEC), SPEC)
                    re_ref[lo + c, :, cols] = out[:SPEC, h * SPEC : (h + 1) * SPEC]
                    im_ref[lo + c, :, cols] = out[SPEC:, h * SPEC : (h + 1) * SPEC]
            return carry

        size = blocks[own].shape[0]
        lax.fori_loop(0, size, one, 0, unroll=4)
        if len(refs) > 2:
            for k, (src, dst) in enumerate(((re_ref, re_out), (im_ref, im_out))):
                for c in range(lo, lo + size):
                    copies.append(pltpu.make_async_copy(src.at[c], dst.at[c], sem.at[k, c]))
                    copies[-1].start()
    for copy in copies:
        copy.wait()


def correlate(place, plan, blocks, so_far=None):
    shape = jax.ShapeDtypeStruct((CH, SPEC, SPEC * GROUPS), BF16)
    vmem = pl.BlockSpec(memory_space=pltpu.VMEM)
    count = len(blocks)
    second = so_far is not None
    operands = [place] + list(blocks) + list(so_far or ())
    out = pl.pallas_call(
        lambda *refs: correlate_kernel(plan, count, *refs),
        out_shape=[shape] * (4 if second else 2),
        in_specs=[pl.BlockSpec(memory_space=pltpu.SMEM)] + [vmem] * (len(operands) - 1),
        out_specs=[vmem] * 2 + [pl.BlockSpec(memory_space=pl.ANY)] * (2 if second else 0),
        scratch_shapes=[pltpu.SemaphoreType.DMA((2, CH))] if second else [],
        input_output_aliases={1 + count: 0, 2 + count: 1} if second else {},
        compiler_params=pltpu.CompilerParams(vmem_limit_bytes=16 * MIB),
        cost_estimate=LIGHT,
        name="correlate",
    )(*operands)
    return out[-2:]


def last_kernel(parts, place_ref, *refs):
    blocks = refs[: 2 * parts]
    re_out, im_out, re_ref, im_ref, sem = refs[-5:]
    cols = pl.ds(pl.multiple_of(place_ref[5], SPEC), SPEC)
    copies, at = [], 0
    for k in range(parts):
        own_ref, other_ref = blocks[2 * k : 2 * k + 2]
        for c in range(own_ref.shape[0]):
            out = products(own_ref[c], other_ref[c])
            re_ref[at + c], im_ref[at + c] = out[:SPEC], out[SPEC:]
        for c in range(at, at + own_ref.shape[0]):
            for k2, (src, dst) in enumerate(((re_ref, re_out), (im_ref, im_out))):
                copies.append(pltpu.make_async_copy(src.at[c], dst.at[c, :, cols], sem.at[k2, c]))
                copies[-1].start()
        at += own_ref.shape[0]
    for copy in copies:
        copy.wait()


def correlate_last(place, blocks, done):
    shape = jax.ShapeDtypeStruct((CH, SPEC, SPEC * GROUPS), BF16)
    vmem, anywhere = pl.BlockSpec(memory_space=pltpu.VMEM), pl.BlockSpec(memory_space=pl.ANY)
    count = len(blocks)
    return pl.pallas_call(
        lambda *refs: last_kernel(count // 2, *refs),
        out_shape=[shape] * 2,
        in_specs=[pl.BlockSpec(memory_space=pltpu.SMEM)] + [vmem] * count + [anywhere] * 2,
        out_specs=[anywhere] * 2,
        scratch_shapes=[pltpu.VMEM((CH, SPEC, SPEC), BF16)] * 2 + [pltpu.SemaphoreType.DMA((2, CH))],
        input_output_aliases={1 + count: 0, 2 + count: 1},
        compiler_params=pltpu.CompilerParams(vmem_limit_bytes=8 * MIB),
        cost_estimate=LIGHT,
        name="correlate_last",
    )(place, *blocks, *done)


def shift(value, axis, by):
    size = lax.axis_size(axis)
    return lax.ppermute(value, axis, [(i, (i + by) % size) for i in range(size)])


def up(value):
    return shift(value, "x", 1)


def down(value):
    return shift(value, "x", -1)


def across(value):
    return shift(value, "z_lo", 1)


def after(values, done):
    return lax.optimization_barrier((values, done))


def on_device(samples, window):
    x, z = lax.axis_index("x"), lax.axis_index("z_lo")
    place = jnp.stack([((x + dx) % 4 * 2 + (z + dz) % 2) * SPEC for dx in range(4) for dz in range(2)]).astype(jnp.int32)

    pieces = filter_and_transform(samples, window, table_rows(0, CH))
    arrived = lax.all_to_all(pieces, FREQ, split_axis=0, concat_axis=0, tiled=True)
    a, b = assemble(arrived, (EARLY, CH - EARLY))
    b_m, b_p, za = up(b), down(b), across(a)
    a_m, a_p, zb = up(a), down(a), across(b)
    (za, b_p, b_m), _ = after((za, b_p, b_m), (za, b_p, b_m))
    za_m, b_o, zb_m = up(za), down(b_p), across(b_m)
    za_p = down(after(za, b_o)[0])
    a_o, zb_p = up(a_m), across(b_p)
    out = correlate(
        place,
        (
            (0, 0, ((0, 0), (2, 1), (3, 6), (4, 2))),
            (EARLY, 1, ((1, 0), (5, 1), (6, 6), (7, 2))),
        ),
        (a, b, za, a_m, a_p, zb, b_m, b_p),
    )
    (za_m, b_o), out = after((za_m, b_o), out)
    za_o, zb_o = up(za_m), across(b_o)
    out = correlate(
        place,
        (
            (0, 0, ((2, 7), (3, 3), (4, 4))),
            (EARLY, 1, ((5, 7), (6, 3), (7, 4))),
        ),
        (a, b, za_m, za_p, a_o, zb_m, zb_p, b_o),
        out,
    )
    return tuple(correlate_last(place, (a, za_o, b, zb_o), out))


def solution(mesh):
    axes = ("x", "z_lo") + FREQ
    fine = Mesh(mesh.devices.reshape(4, 2, 4, 4, 2), axes)
    return jax.shard_map(
        on_device,
        mesh=fine,
        in_specs=(P(axes, None), P()),
        out_specs=(P(FREQ, axes[:2], None), P(FREQ, axes[:2], None)),
        check_vma=False,
    )
```

```python
import math

import jax
import jax.numpy as jnp
import ml_dtypes
import numpy as np
from jax import lax
from jax.experimental import pallas as pl
from jax.experimental.pallas import tpu as pltpu
from jax.sharding import Mesh, PartitionSpec as P

CHAN = 512
NFFT = 2048
TAPS = 4
SPEC = 128
FRAMES = SPEC + TAPS - 1
ROWS_IN = 4
GROUPS = 8
N_FREQ = 32
CH = CHAN // N_FREQ
LANES = 128
SUB = 8
F32 = jnp.float32
BF16 = jnp.bfloat16
NT = (((1,), (1,)), ((), ()))
MIB = 1 << 20
FREQ = ("y", "z_hi", "core")
LIGHT = pl.CostEstimate(flops=1000, bytes_accessed=1000, transcendentals=0)

EARLY = 9
HALF = 4


def table_rows(lo, count):
    j = np.arange(NFFT, dtype=np.int64)
    c = (np.arange(N_FREQ)[:, None] * CH + lo + np.arange(count)[None, :]).reshape(-1)
    angle = ((c[:, None] * j[None, :]) % NFFT).astype(np.float32) * np.float32(2.0 * math.pi / NFFT)
    both = np.stack([np.cos(angle), -np.sin(angle)], axis=0)
    both = both.reshape(2, N_FREQ, count, NFFT).transpose(1, 0, 2, 3)
    return jnp.asarray(both.reshape(2 * N_FREQ * count, NFFT).astype(ml_dtypes.bfloat16))


def store_spectra(raw, o_ref, first, per):
    out = (raw * (1.0 / math.sqrt(NFFT))).astype(BF16)
    for d in range(raw.shape[0] // per):
        for i in range(ROWS_IN):
            o_ref[first + d, i] = out[d * per : (d + 1) * per, i * SPEC : (i + 1) * SPEC]


def filter_kernel(rows, s_hbm, w_ref, t_hbm, o_ref, s_ref, t_ref, f_ref, wv_ref, s_sem, t_sem):
    parts = 4
    span = SPEC // parts
    edges = [0] + [(h + 1) * span + TAPS - 1 for h in range(parts)]
    arrivals = []
    for h in range(parts):
        cut = pl.ds(edges[h], edges[h + 1] - edges[h])
        arrivals.append(pltpu.make_async_copy(s_hbm.at[cut], s_ref.at[cut], s_sem.at[h]))
    for copy in arrivals:
        copy.start()
    table_copy = pltpu.make_async_copy(t_hbm, t_ref, t_sem)
    table_copy.start()
    pairs = NFFT // LANES // 2
    for a in range(pairs):
        for t in range(TAPS):
            halves = [
                jnp.broadcast_to(w_ref[t : t + 1, (2 * a + b) * LANES : (2 * a + b + 1) * LANES] * (1.0 / 64.0), (ROWS_IN, LANES))
                for b in range(2)
            ]
            wv_ref[a, t] = jnp.concatenate(halves, axis=0)
    for h in range(parts):
        arrivals[h].wait()

        def step(a, carry):
            sub = pl.ds(pl.multiple_of(a * SUB, SUB), SUB)
            taps = [wv_ref[a, t] for t in range(TAPS)]
            for s0 in range(h * span, (h + 1) * span, 2 * SUB):
                v = [s_ref[s0 + k, sub, :].astype(F32) for k in range(2 * SUB + TAPS - 1)]
                sums = []
                for k in range(2 * SUB):
                    acc = taps[0] * v[k]
                    for t in range(1, TAPS):
                        acc = acc + taps[t] * v[k + t]
                    sums.append(acc)
                low = jnp.swapaxes(jnp.stack(sums[:SUB], axis=0), 0, 1)
                high = jnp.swapaxes(jnp.stack(sums[SUB:], axis=0), 0, 1)
                both = jnp.concatenate([low, high], axis=1).astype(BF16)
                for b in range(2):
                    lane = pl.ds(pl.multiple_of((2 * a + b) * LANES, LANES), LANES)
                    for i in range(ROWS_IN):
                        f_ref[i * SPEC + s0 : i * SPEC + s0 + 2 * SUB, lane] = both[b * ROWS_IN + i]
            return carry

        lax.fori_loop(0, pairs, step, 0)
    table_copy.wait()
    tile = 256
    per = rows // N_FREQ
    for m in range(rows // tile):
        raw = lax.dot_general(t_ref[m * tile : (m + 1) * tile, :], f_ref[...], NT, preferred_element_type=F32)
        store_spectra(raw, o_ref, m * (tile // per), per)


def filter_and_transform(samples, window, table):
    view = samples.reshape(ROWS_IN, FRAMES, NFFT // LANES, LANES).transpose(1, 2, 0, 3)
    view = view.reshape(FRAMES, NFFT // LANES * ROWS_IN, LANES)
    rows = table.shape[0]
    return pl.pallas_call(
        lambda *refs: filter_kernel(rows, *refs),
        out_shape=jax.ShapeDtypeStruct((N_FREQ, ROWS_IN, rows // N_FREQ, SPEC), BF16),
        in_specs=[
            pl.BlockSpec(memory_space=pl.ANY),
            pl.BlockSpec(memory_space=pltpu.VMEM),
            pl.BlockSpec(memory_space=pl.ANY),
        ],
        out_specs=pl.BlockSpec(memory_space=pltpu.VMEM),
        scratch_shapes=[
            pltpu.VMEM((FRAMES, NFFT // LANES * ROWS_IN, LANES), jnp.int32),
            pltpu.VMEM((rows, NFFT), BF16),
            pltpu.VMEM((ROWS_IN * SPEC, NFFT), BF16),
            pltpu.VMEM((NFFT // LANES // 2, TAPS, SUB, LANES), F32),
            pltpu.SemaphoreType.DMA((4,)),
            pltpu.SemaphoreType.DMA,
        ],
        compiler_params=pltpu.CompilerParams(vmem_limit_bytes=60 * MIB),
        cost_estimate=LIGHT,
        name="filter_and_transform",
    )(view, window, table)


def assemble_kernel(sizes, x_ref, *refs):
    outs, wide = refs[:-1], refs[-1]
    count, pitch = sum(sizes), wide.shape[1]
    wide[:, : 2 * count, :] = x_ref[...].astype(F32)
    flat = wide.reshape(SPEC * pitch, SPEC)
    lo = 0
    for out, size in zip(outs, sizes):
        for c in range(size):
            for p in range(2):
                rows = pl.ds(p * count + lo + c, SPEC, stride=pitch)
                out[c, :, p * SPEC : (p + 1) * SPEC] = flat[rows, :].astype(BF16)
        lo += size


def assemble(pieces, sizes):
    count = sum(sizes)
    pitch = 2 * count + SUB if 2 * count // SUB % 2 == 0 else 2 * count
    return pl.pallas_call(
        lambda *refs: assemble_kernel(sizes, *refs),
        out_shape=[jax.ShapeDtypeStruct((size, SPEC, 2 * SPEC), BF16) for size in sizes],
        scratch_shapes=[pltpu.VMEM((SPEC, pitch, SPEC), F32)],
        compiler_params=pltpu.CompilerParams(vmem_limit_bytes=8 * MIB),
        cost_estimate=LIGHT,
        name="assemble",
    )(pieces.reshape(SPEC, 2 * count, SPEC))


def products(own, other):
    rotated = jnp.concatenate([own[:, SPEC:], -own[:, :SPEC]], axis=1)
    left = jnp.concatenate([own, rotated], axis=0)
    return (lax.dot_general(left, other, NT, preferred_element_type=F32) * (1.0 / SPEC)).astype(BF16)


def correlate_kernel(plan, count, place_ref, *refs):
    blocks, refs = refs[:count], refs[count:]
    copies = []
    if len(refs) == 2:
        re_ref, im_ref = refs
    else:
        re_ref, im_ref, re_out, im_out, sem = refs[-5:]
    for lo, own, others in plan:

        def one(c, carry):
            for k in range(0, len(others), 2):
                pair = others[k : k + 2]
                right = jnp.concatenate([blocks[b][c] for b, _ in pair], axis=0)
                out = products(blocks[own][c], right)
                for h, (_, spot) in enumerate(pair):
                    cols = pl.ds(pl.multiple_of(place_ref[spot], SPEC), SPEC)
                    re_ref[lo + c, :, cols] = out[:SPEC, h * SPEC : (h + 1) * SPEC]
                    im_ref[lo + c, :, cols] = out[SPEC:, h * SPEC : (h + 1) * SPEC]
            return carry

        size = blocks[own].shape[0]
        lax.fori_loop(0, size, one, 0, unroll=4)
        if len(refs) > 2:
            for k, (src, dst) in enumerate(((re_ref, re_out), (im_ref, im_out))):
                for c in range(lo, lo + size):
                    copies.append(pltpu.make_async_copy(src.at[c], dst.at[c], sem.at[k, c]))
                    copies[-1].start()
    for copy in copies:
        copy.wait()


def correlate(place, plan, blocks, so_far=None):
    shape = jax.ShapeDtypeStruct((CH, SPEC, SPEC * GROUPS), BF16)
    vmem = pl.BlockSpec(memory_space=pltpu.VMEM)
    count = len(blocks)
    second = so_far is not None
    operands = [place] + list(blocks) + list(so_far or ())
    out = pl.pallas_call(
        lambda *refs: correlate_kernel(plan, count, *refs),
        out_shape=[shape] * (4 if second else 2),
        in_specs=[pl.BlockSpec(memory_space=pltpu.SMEM)] + [vmem] * (len(operands) - 1),
        out_specs=[vmem] * 2 + [pl.BlockSpec(memory_space=pl.ANY)] * (2 if second else 0),
        scratch_shapes=[pltpu.SemaphoreType.DMA((2, CH))] if second else [],
        input_output_aliases={1 + count: 0, 2 + count: 1} if second else {},
        compiler_params=pltpu.CompilerParams(vmem_limit_bytes=16 * MIB),
        cost_estimate=LIGHT,
        name="correlate",
    )(*operands)
    return out[-2:]


def last_kernel(plan, count, place_ref, *refs):
    blocks = refs[:count]
    re_out, im_out, re_ref, im_ref, sem = refs[-5:]
    cols = pl.ds(pl.multiple_of(place_ref[5], SPEC), SPEC)
    copies, at = [], 0
    for own, first, other in plan:
        own_ref, other_ref = blocks[own], blocks[other]
        size = other_ref.shape[0]
        for c in range(size):
            out = products(own_ref[first + c], other_ref[c])
            re_ref[at + c], im_ref[at + c] = out[:SPEC], out[SPEC:]
        for c in range(at, at + size):
            for k2, (src, dst) in enumerate(((re_ref, re_out), (im_ref, im_out))):
                copies.append(pltpu.make_async_copy(src.at[c], dst.at[c, :, cols], sem.at[k2, c]))
                copies[-1].start()
        at += size
    for copy in copies:
        copy.wait()


def correlate_last(place, plan, blocks, done):
    shape = jax.ShapeDtypeStruct((CH, SPEC, SPEC * GROUPS), BF16)
    vmem, anywhere = pl.BlockSpec(memory_space=pltpu.VMEM), pl.BlockSpec(memory_space=pl.ANY)
    count = len(blocks)
    return pl.pallas_call(
        lambda *refs: last_kernel(plan, count, *refs),
        out_shape=[shape] * 2,
        in_specs=[pl.BlockSpec(memory_space=pltpu.SMEM)] + [vmem] * count + [anywhere] * 2,
        out_specs=[anywhere] * 2,
        scratch_shapes=[pltpu.VMEM((CH, SPEC, SPEC), BF16)] * 2 + [pltpu.SemaphoreType.DMA((2, CH))],
        input_output_aliases={1 + count: 0, 2 + count: 1},
        compiler_params=pltpu.CompilerParams(vmem_limit_bytes=8 * MIB),
        cost_estimate=LIGHT,
        name="correlate_last",
    )(place, *blocks, *done)


def shift(value, axis, by):
    size = lax.axis_size(axis)
    return lax.ppermute(value, axis, [(i, (i + by) % size) for i in range(size)])


def up(value):
    return shift(value, "x", 1)


def down(value):
    return shift(value, "x", -1)


def across(value):
    return shift(value, "z_lo", 1)


def after(values, done):
    return lax.optimization_barrier((values, done))


def on_device(samples, window):
    x, z = lax.axis_index("x"), lax.axis_index("z_lo")
    place = jnp.stack([((x + dx) % 4 * 2 + (z + dz) % 2) * SPEC for dx in range(4) for dz in range(2)]).astype(jnp.int32)

    pieces = filter_and_transform(samples, window, table_rows(0, CH))
    arrived = lax.all_to_all(pieces, FREQ, split_axis=0, concat_axis=0, tiled=True)
    a, b = assemble(arrived, (EARLY, CH - EARLY))
    b_m, b_p, za = up(b), down(b), across(a)
    a_m, a_p, zb = up(a), down(a), across(b)
    (za, b_p, b_m), _ = after((za, b_p, b_m), (za, b_p, b_m))
    za_m, b_o, zb_m = up(za), down(b_p), across(b_m)
    a_o, za_p, zb_p = up(a_m), down(za), across(b_p)
    out = correlate(
        place,
        (
            (0, 0, ((0, 0), (2, 1), (3, 6), (4, 2))),
            (EARLY, 1, ((1, 0), (5, 1), (6, 6), (7, 2))),
        ),
        (a, b, za, a_m, a_p, zb, b_m, b_p),
    )
    (za_m, b_o), out = after((za_m, b_o), out)
    za_lo, zb_o = up(za_m[:HALF]), across(b_o)
    za_hi = down(za_p[HALF:])
    out = correlate(
        place,
        (
            (0, 0, ((2, 7), (3, 3), (4, 4))),
            (EARLY, 1, ((5, 7), (6, 3), (7, 4))),
        ),
        (a, b, za_m, za_p, a_o, zb_m, zb_p, b_o),
        out,
    )
    plan = ((0, 0, 2), (0, HALF, 3), (1, 0, 4))
    return tuple(correlate_last(place, plan, (a, b, za_lo, za_hi, zb_o), out))


def solution(mesh):
    axes = ("x", "z_lo") + FREQ
    fine = Mesh(mesh.devices.reshape(4, 2, 4, 4, 2), axes)
    return jax.shard_map(
        on_device,
        mesh=fine,
        in_specs=(P(axes, None), P()),
        out_specs=(P(FREQ, axes[:2], None), P(FREQ, axes[:2], None)),
        check_vma=False,
    )
```

```python
import math

import jax
import jax.numpy as jnp
import ml_dtypes
import numpy as np
from jax import lax
from jax.experimental import pallas as pl
from jax.experimental.pallas import tpu as pltpu
from jax.sharding import Mesh, PartitionSpec as P

CHAN = 512
NFFT = 2048
TAPS = 4
SPEC = 128
FRAMES = SPEC + TAPS - 1
ROWS_IN = 4
GROUPS = 8
N_FREQ = 32
CH = CHAN // N_FREQ
LANES = 128
SUB = 8
F32 = jnp.float32
BF16 = jnp.bfloat16
NT = (((1,), (1,)), ((), ()))
MIB = 1 << 20
FREQ = ("y", "z_hi", "core")
LIGHT = pl.CostEstimate(flops=1000, bytes_accessed=1000, transcendentals=0)

EARLY = 9
HALF = 5


def table_rows(lo, count):
    j = np.arange(NFFT, dtype=np.int64)
    c = (np.arange(N_FREQ)[:, None] * CH + lo + np.arange(count)[None, :]).reshape(-1)
    angle = ((c[:, None] * j[None, :]) % NFFT).astype(np.float32) * np.float32(2.0 * math.pi / NFFT)
    both = np.stack([np.cos(angle), -np.sin(angle)], axis=0)
    both = both.reshape(2, N_FREQ, count, NFFT).transpose(1, 0, 2, 3)
    return jnp.asarray(both.reshape(2 * N_FREQ * count, NFFT).astype(ml_dtypes.bfloat16))


def store_spectra(raw, o_ref, first, per):
    out = (raw * (1.0 / math.sqrt(NFFT))).astype(BF16)
    for d in range(raw.shape[0] // per):
        for i in range(ROWS_IN):
            o_ref[first + d, i] = out[d * per : (d + 1) * per, i * SPEC : (i + 1) * SPEC]


def filter_kernel(rows, s_hbm, w_ref, t_hbm, o_ref, s_ref, t_ref, f_ref, wv_ref, s_sem, t_sem):
    parts = 4
    span = SPEC // parts
    edges = [0] + [(h + 1) * span + TAPS - 1 for h in range(parts)]
    arrivals = []
    for h in range(parts):
        cut = pl.ds(edges[h], edges[h + 1] - edges[h])
        arrivals.append(pltpu.make_async_copy(s_hbm.at[cut], s_ref.at[cut], s_sem.at[h]))
    for copy in arrivals:
        copy.start()
    table_copy = pltpu.make_async_copy(t_hbm, t_ref, t_sem)
    table_copy.start()
    pairs = NFFT // LANES // 2
    for a in range(pairs):
        for t in range(TAPS):
            halves = [
                jnp.broadcast_to(w_ref[t : t + 1, (2 * a + b) * LANES : (2 * a + b + 1) * LANES] * (1.0 / 64.0), (ROWS_IN, LANES))
                for b in range(2)
            ]
            wv_ref[a, t] = jnp.concatenate(halves, axis=0)
    for h in range(parts):
        arrivals[h].wait()

        def step(a, carry):
            sub = pl.ds(pl.multiple_of(a * SUB, SUB), SUB)
            taps = [wv_ref[a, t] for t in range(TAPS)]
            for s0 in range(h * span, (h + 1) * span, 2 * SUB):
                v = [s_ref[s0 + k, sub, :].astype(F32) for k in range(2 * SUB + TAPS - 1)]
                sums = []
                for k in range(2 * SUB):
                    acc = taps[0] * v[k]
                    for t in range(1, TAPS):
                        acc = acc + taps[t] * v[k + t]
                    sums.append(acc)
                low = jnp.swapaxes(jnp.stack(sums[:SUB], axis=0), 0, 1)
                high = jnp.swapaxes(jnp.stack(sums[SUB:], axis=0), 0, 1)
                both = jnp.concatenate([low, high], axis=1).astype(BF16)
                for b in range(2):
                    lane = pl.ds(pl.multiple_of((2 * a + b) * LANES, LANES), LANES)
                    for i in range(ROWS_IN):
                        f_ref[i * SPEC + s0 : i * SPEC + s0 + 2 * SUB, lane] = both[b * ROWS_IN + i]
            return carry

        lax.fori_loop(0, pairs, step, 0)
    table_copy.wait()
    tile = 256
    per = rows // N_FREQ
    for m in range(rows // tile):
        raw = lax.dot_general(t_ref[m * tile : (m + 1) * tile, :], f_ref[...], NT, preferred_element_type=F32)
        store_spectra(raw, o_ref, m * (tile // per), per)


def filter_and_transform(samples, window, table):
    view = samples.reshape(ROWS_IN, FRAMES, NFFT // LANES, LANES).transpose(1, 2, 0, 3)
    view = view.reshape(FRAMES, NFFT // LANES * ROWS_IN, LANES)
    rows = table.shape[0]
    return pl.pallas_call(
        lambda *refs: filter_kernel(rows, *refs),
        out_shape=jax.ShapeDtypeStruct((N_FREQ, ROWS_IN, rows // N_FREQ, SPEC), BF16),
        in_specs=[
            pl.BlockSpec(memory_space=pl.ANY),
            pl.BlockSpec(memory_space=pltpu.VMEM),
            pl.BlockSpec(memory_space=pl.ANY),
        ],
        out_specs=pl.BlockSpec(memory_space=pltpu.VMEM),
        scratch_shapes=[
            pltpu.VMEM((FRAMES, NFFT // LANES * ROWS_IN, LANES), jnp.int32),
            pltpu.VMEM((rows, NFFT), BF16),
            pltpu.VMEM((ROWS_IN * SPEC, NFFT), BF16),
            pltpu.VMEM((NFFT // LANES // 2, TAPS, SUB, LANES), F32),
            pltpu.SemaphoreType.DMA((4,)),
            pltpu.SemaphoreType.DMA,
        ],
        compiler_params=pltpu.CompilerParams(vmem_limit_bytes=60 * MIB),
        cost_estimate=LIGHT,
        name="filter_and_transform",
    )(view, window, table)


def assemble_kernel(sizes, x_ref, *refs):
    outs, wide = refs[:-1], refs[-1]
    count, pitch = sum(sizes), wide.shape[1]
    wide[:, : 2 * count, :] = x_ref[...].astype(F32)
    flat = wide.reshape(SPEC * pitch, SPEC)
    lo = 0
    for out, size in zip(outs, sizes):
        for c in range(size):
            for p in range(2):
                rows = pl.ds(p * count + lo + c, SPEC, stride=pitch)
                out[c, :, p * SPEC : (p + 1) * SPEC] = flat[rows, :].astype(BF16)
        lo += size


def assemble(pieces, sizes):
    count = sum(sizes)
    pitch = 2 * count + SUB if 2 * count // SUB % 2 == 0 else 2 * count
    return pl.pallas_call(
        lambda *refs: assemble_kernel(sizes, *refs),
        out_shape=[jax.ShapeDtypeStruct((size, SPEC, 2 * SPEC), BF16) for size in sizes],
        scratch_shapes=[pltpu.VMEM((SPEC, pitch, SPEC), F32)],
        compiler_params=pltpu.CompilerParams(vmem_limit_bytes=8 * MIB),
        cost_estimate=LIGHT,
        name="assemble",
    )(pieces.reshape(SPEC, 2 * count, SPEC))


def products(own, other):
    rotated = jnp.concatenate([own[:, SPEC:], -own[:, :SPEC]], axis=1)
    left = jnp.concatenate([own, rotated], axis=0)
    return (lax.dot_general(left, other, NT, preferred_element_type=F32) * (1.0 / SPEC)).astype(BF16)


def correlate_kernel(plan, count, place_ref, *refs):
    blocks, refs = refs[:count], refs[count:]
    copies = []
    if len(refs) == 2:
        re_ref, im_ref = refs
    else:
        re_ref, im_ref, re_out, im_out, sem = refs[-5:]
    for lo, own, others in plan:

        def one(c, carry):
            for k in range(0, len(others), 2):
                pair = others[k : k + 2]
                right = jnp.concatenate([blocks[b][c] for b, _ in pair], axis=0)
                out = products(blocks[own][c], right)
                for h, (_, spot) in enumerate(pair):
                    cols = pl.ds(pl.multiple_of(place_ref[spot], SPEC), SPEC)
                    re_ref[lo + c, :, cols] = out[:SPEC, h * SPEC : (h + 1) * SPEC]
                    im_ref[lo + c, :, cols] = out[SPEC:, h * SPEC : (h + 1) * SPEC]
            return carry

        size = blocks[own].shape[0]
        lax.fori_loop(0, size, one, 0, unroll=4)
        if len(refs) > 2:
            for k, (src, dst) in enumerate(((re_ref, re_out), (im_ref, im_out))):
                for c in range(lo, lo + size):
                    copies.append(pltpu.make_async_copy(src.at[c], dst.at[c], sem.at[k, c]))
                    copies[-1].start()
    for copy in copies:
        copy.wait()


def correlate(place, plan, blocks, so_far=None):
    shape = jax.ShapeDtypeStruct((CH, SPEC, SPEC * GROUPS), BF16)
    vmem = pl.BlockSpec(memory_space=pltpu.VMEM)
    count = len(blocks)
    second = so_far is not None
    operands = [place] + list(blocks) + list(so_far or ())
    out = pl.pallas_call(
        lambda *refs: correlate_kernel(plan, count, *refs),
        out_shape=[shape] * (4 if second else 2),
        in_specs=[pl.BlockSpec(memory_space=pltpu.SMEM)] + [vmem] * (len(operands) - 1),
        out_specs=[vmem] * 2 + [pl.BlockSpec(memory_space=pl.ANY)] * (2 if second else 0),
        scratch_shapes=[pltpu.SemaphoreType.DMA((2, CH))] if second else [],
        input_output_aliases={1 + count: 0, 2 + count: 1} if second else {},
        compiler_params=pltpu.CompilerParams(vmem_limit_bytes=16 * MIB),
        cost_estimate=LIGHT,
        name="correlate",
    )(*operands)
    return out[-2:]


def last_kernel(plan, count, place_ref, *refs):
    blocks = refs[:count]
    re_out, im_out, re_ref, im_ref, sem = refs[-5:]
    cols = pl.ds(pl.multiple_of(place_ref[5], SPEC), SPEC)
    copies, at = [], 0
    for own, first, other in plan:
        own_ref, other_ref = blocks[own], blocks[other]
        size = other_ref.shape[0]
        for c in range(size):
            out = products(own_ref[first + c], other_ref[c])
            re_ref[at + c], im_ref[at + c] = out[:SPEC], out[SPEC:]
        for c in range(at, at + size):
            for k2, (src, dst) in enumerate(((re_ref, re_out), (im_ref, im_out))):
                copies.append(pltpu.make_async_copy(src.at[c], dst.at[c, :, cols], sem.at[k2, c]))
                copies[-1].start()
        at += size
    for copy in copies:
        copy.wait()


def correlate_last(place, plan, blocks, done):
    shape = jax.ShapeDtypeStruct((CH, SPEC, SPEC * GROUPS), BF16)
    vmem, anywhere = pl.BlockSpec(memory_space=pltpu.VMEM), pl.BlockSpec(memory_space=pl.ANY)
    count = len(blocks)
    return pl.pallas_call(
        lambda *refs: last_kernel(plan, count, *refs),
        out_shape=[shape] * 2,
        in_specs=[pl.BlockSpec(memory_space=pltpu.SMEM)] + [vmem] * count + [anywhere] * 2,
        out_specs=[anywhere] * 2,
        scratch_shapes=[pltpu.VMEM((CH, SPEC, SPEC), BF16)] * 2 + [pltpu.SemaphoreType.DMA((2, CH))],
        input_output_aliases={1 + count: 0, 2 + count: 1},
        compiler_params=pltpu.CompilerParams(vmem_limit_bytes=8 * MIB),
        cost_estimate=LIGHT,
        name="correlate_last",
    )(place, *blocks, *done)


def shift(value, axis, by):
    size = lax.axis_size(axis)
    return lax.ppermute(value, axis, [(i, (i + by) % size) for i in range(size)])


def up(value):
    return shift(value, "x", 1)


def down(value):
    return shift(value, "x", -1)


def across(value):
    return shift(value, "z_lo", 1)


def after(values, done):
    return lax.optimization_barrier((values, done))


def on_device(samples, window):
    x, z = lax.axis_index("x"), lax.axis_index("z_lo")
    place = jnp.stack([((x + dx) % 4 * 2 + (z + dz) % 2) * SPEC for dx in range(4) for dz in range(2)]).astype(jnp.int32)

    pieces = filter_and_transform(samples, window, table_rows(0, CH))
    arrived = lax.all_to_all(pieces, FREQ, split_axis=0, concat_axis=0, tiled=True)
    a, b = assemble(arrived, (EARLY, CH - EARLY))
    b_m, b_p, za = up(b), down(b), across(a)
    a_m, a_p, zb = up(a), down(a), across(b)
    (za, b_p, b_m), _ = after((za, b_p, b_m), (za, b_p, b_m))
    za_m, b_o, zb_m = up(za), down(b_p), across(b_m)
    a_o, za_p, zb_p = up(a_m), down(za), across(b_p)
    out = correlate(
        place,
        (
            (0, 0, ((0, 0), (2, 1), (3, 6), (4, 2))),
            (EARLY, 1, ((1, 0), (5, 1), (6, 6), (7, 2))),
        ),
        (a, b, za, a_m, a_p, zb, b_m, b_p),
    )
    (za_m, b_o), out = after((za_m, b_o), out)
    za_lo, zb_o = up(za_m[:HALF]), across(b_o)
    za_hi = down(za_p[HALF:])
    out = correlate(
        place,
        (
            (0, 0, ((2, 7), (3, 3), (4, 4))),
            (EARLY, 1, ((5, 7), (6, 3), (7, 4))),
        ),
        (a, b, za_m, za_p, a_o, zb_m, zb_p, b_o),
        out,
    )
    plan = ((0, 0, 2), (0, HALF, 3), (1, 0, 4))
    return tuple(correlate_last(place, plan, (a, b, za_lo, za_hi, zb_o), out))


def solution(mesh):
    axes = ("x", "z_lo") + FREQ
    fine = Mesh(mesh.devices.reshape(4, 2, 4, 4, 2), axes)
    return jax.shard_map(
        on_device,
        mesh=fine,
        in_specs=(P(axes, None), P()),
        out_specs=(P(FREQ, axes[:2], None), P(FREQ, axes[:2], None)),
        check_vma=False,
    )
```
